768 devices in a mesh: replica: 96 (over y_hi, z, core), fsdp: 8 (over x, y_lo).
Axes of the slice: x: 4, y: 8 (y_hi: 4, y_lo: 2; y = y_hi * 2 + y_lo), z: 12, core: 2. Of those that a mesh axis runs over, the one named last changes fastest.
Arguments:
- local_params: float32 [96, 48, 8192], P('replica', 'fsdp'), may hold values from -6 to 6
- global_params: float32 [48, 8192], P('fsdp'), may hold values from -6 to 6
- momentum: float32 [48, 8192], P('fsdp'), may hold values from -6 to 6
- layer_input: bfloat16 [96, 1024, 512], P('replica', 'fsdp'), may hold values from -6 to 6
- output_grad: bfloat16 [96, 1024, 8192], P('replica', 'fsdp'), may hold values from -0.1875 to 0.1875
- token_ids: int32 [96, 1024], P('replica', 'fsdp'), may hold values from 0 to 65023, as said below
Outputs:
- new_global: float32 [48, 8192], P('fsdp')
- new_momentum: float32 [48, 8192], P('fsdp')
- inner_grad: bfloat16 [96, 512, 8192], P('replica', 'fsdp')
The draws below stay inside these ranges and needn't reach their ends.
Inputs may be any that keep to these rules, and one draw needn't show every extreme that they name: `token_ids`: id 0 is padding; it fills a tail of 1 to 256 positions of each of a replica's 2 sequences, and no other position.
All inputs are finite; a program needn't handle non-finite values.
Results may differ from the reference program's by a relative error of at most 0.017.
Values may be sent and summed in bfloat16 or wider, within the bound.
A program may use at most 64 MiB of HBM per device.

```python
import jax
import jax.numpy as jnp
from jax import lax

D = 8192
VOCAB = 65024
BLOCK = 128
SEQS = 2
TOK_DEV = 128
R_IN = 512
FRAG_ROWS = 48
TOKENS_R = 1024
N_REPLICA = 96
N_FSDP = 8


def draw_token_ids(key, part):
    key = jax.random.fold_in(key, 7)
    first, second = jax.random.split(key)
    total = TOK_DEV * N_FSDP
    length = total // SEQS
    tokens = jax.random.randint(first, (N_REPLICA, total), 1, VOCAB)
    tail = jax.random.randint(second, (N_REPLICA, SEQS, 1), 1, length // 2 + 1)
    position = jnp.arange(length)[None, None, :]
    padded = (position >= length - tail).reshape(N_REPLICA, total)
    tokens = jnp.where(padded, 0, tokens)
    tokens = tokens.at[0, 0].set(VOCAB - 1)
    return tokens.astype(jnp.int32)


def with_spikes(result, key, source, target, shards_of, factor):
    def block_of(dim):
        return (jnp.arange(result.shape[dim]) // (result.shape[dim] // shards_of)).reshape((-1,) + (1,) * (result.ndim - 1 - dim))

    near = jax.random.permutation(key, shards_of)[block_of(target)]
    second = (block_of(target) + shards_of // 2) % shards_of
    return jnp.where((block_of(source) == near) | (block_of(source) == second), factor * result, result)


def steps_of(stream_key, extent, cuts, low, largest):
    level = 1.0
    for dim, shards_of in cuts:
        draws = jax.random.uniform(jax.random.fold_in(jax.random.fold_in(stream_key, 6), dim), (shards_of,), jnp.float32, low / len(cuts), largest / len(cuts))
        level = level * jnp.repeat(jnp.exp(draws), extent[dim] // shards_of).reshape((-1,) + (1,) * (len(extent) - 1 - dim))
    return level


def normal_values(key, shape, deviation, reach, pieces=(), kind=jnp.bfloat16):
    level = steps_of(key, shape, pieces, -0.22, 0.18) if pieces else 1.0
    values = jax.random.normal(key, shape, jnp.float32) * deviation * level
    return jnp.minimum(jnp.maximum(values, -reach), reach).astype(kind)


def bell_draw_with(own_key, dims, spread, most, pieces, heavy, held_as=jnp.bfloat16):
    drawn = spread * jax.random.normal(own_key, dims, jnp.float32)
    if pieces:
        drawn = drawn * steps_of(own_key, dims, pieces, -0.22, 0.18)
    return jnp.clip(with_spikes(drawn, jax.random.fold_in(own_key, 3), *heavy), -most, most).astype(held_as)


def setup_inputs(seed: int = 0) -> dict:
    splits = jax.random.split(jax.random.key(seed), 7)
    return {
        "local_params": normal_values(splits[0], (N_REPLICA, FRAG_ROWS, D), 1.0, 6.0, ((0, 96), (1, 8)), jnp.float32),
        "global_params": normal_values(splits[1], (FRAG_ROWS, D), 1.0, 6.0, ((0, 8),), jnp.float32),
        "momentum": normal_values(splits[2], (FRAG_ROWS, D), 0.5, 6.0, ((0, 8),), jnp.float32),
        "layer_input": bell_draw_with(splits[3], (N_REPLICA, TOKENS_R, R_IN), 1.0, 6.0, ((0, 96), (1, 8)), (1, 2, 8, 2.0)),
        "output_grad": normal_values(splits[4], (N_REPLICA, TOKENS_R, D), (TOK_DEV * N_FSDP) ** -0.5, 0.1875, ((0, 96), (1, 8))),
        "token_ids": draw_token_ids(jax.random.fold_in(splits[6], 71), 0),
    }


EPS = 1e-6
MU = 0.9
LR = 0.7


def reference(local_params, global_params, momentum, layer_input, output_grad, token_ids):
    delta = global_params[None] - local_params
    blocks = delta.reshape(N_REPLICA, -1, BLOCK)
    scale = (jnp.max(jnp.abs(blocks), axis=2, keepdims=True) + EPS).astype(jnp.bfloat16)
    scale_wide = scale.astype(jnp.float32)
    codes = (blocks / scale_wide).astype(jnp.bfloat16)
    values = codes.astype(jnp.float32) * scale_wide
    average = (jnp.sum(values, axis=0) / N_REPLICA).reshape(FRAG_ROWS, D)
    new_momentum = MU * momentum + average
    new_global = global_params - LR * (average + MU * new_momentum)
    keep = (token_ids != 0)[:, :, None]
    masked = jnp.where(keep, output_grad, jnp.zeros((), jnp.bfloat16))

    def one_replica(pair):
        inputs, grads = pair
        inputs_wide = inputs.reshape(N_FSDP, TOK_DEV, R_IN).astype(jnp.float32)
        grads_wide = grads.reshape(N_FSDP, TOK_DEV, D).astype(jnp.float32)
        parts = jnp.einsum("ftr,ftd->frd", inputs_wide, grads_wide)
        parts = lax.optimization_barrier(parts.astype(jnp.bfloat16)).astype(jnp.float32)
        return jnp.sum(parts, axis=0).astype(jnp.bfloat16)

    inner_grad = lax.map(one_replica, (layer_input, masked))
    return new_global, new_momentum, inner_grad
```

```python
import functools

import jax
import jax.numpy as jnp
from jax import lax
from jax.experimental import pallas as pl
from jax.experimental.pallas import tpu as pltpu
from jax.sharding import PartitionSpec as P

EPS = 1e-06
MU = 0.9
LR = 0.7
MESH = pl.DeviceIdType.MESH

BLOCK = 128
NX = 4
NY = 2
CHUNKS = 8


def ds(start, size):
    return pl.ds(pl.multiple_of(start, size), size)


def kernel(
    dims,
    local_hbm, global_hbm, momentum_hbm, input_hbm, grad_hbm, ids_hbm,
    new_global_ref, new_momentum_ref, out_ref,
    local_v, global_v, momentum_v, input_v, ids_v,
    global_rows, values, part1, part2, average,
    inputs_t, grads, y_out, y_in, own_half, done,
    load_sem, own_sem, store_sem,
    l_send, l_recv, g_send, g_recv, y_send, y_recv, o_send, o_recv,
    a1_send, a1_recv, a2_send, a2_recv, a3_send, a3_recv,
):
    NYH, NZ, NC = dims
    replica, me = lax.axis_index("replica"), lax.axis_index("fsdp")
    x, y = lax.div(me, NY), lax.rem(me, NY)
    core = lax.rem(replica, NC)
    z = lax.rem(lax.div(replica, NC), NZ)
    yh = lax.div(replica, NC * NZ)

    tokens, d = grad_hbm.shape
    r_in = input_v.shape[1]
    rows = r_in // (NX * NY)
    half = r_in // NY
    cols = d // NX
    w = cols // CHUNKS
    n_blocks = d // BLOCK
    frag = global_v.shape[0]
    n_rows = local_v.shape[0]
    rz = n_rows // NZ

    def x_peer(dx):
        px = lax.rem(x + dx, NX)
        return px, (replica, px * NY + y)

    y_peer = (replica, x * NY + (1 - y))

    def z_peer(dz):
        pz = lax.rem(z + dz, NZ)
        return pz, ((yh * NZ + pz) * NC + core, me)

    group = NYH * NC
    g_me = yh * NC + core

    def g_peer(k):
        pk = lax.rem(g_me + k, group)
        return pk, ((lax.div(pk, NC) * NZ + z) * NC + lax.rem(pk, NC), me)

    loads = [
        pltpu.make_async_copy(src, dst, load_sem.at[i])
        for i, (src, dst) in enumerate(
            [(input_hbm, input_v), (ids_hbm, ids_v), (global_hbm, global_v), (local_hbm, local_v), (momentum_hbm, momentum_v)]
        )
    ]
    for copy in loads:
        copy.start()
    own_grads = pltpu.make_async_copy(
        grad_hbm.at[:, ds(x * cols, cols)], grads.at[ds(x * tokens, tokens), :], own_sem
    )
    own_grads.start()

    barrier = pltpu.get_barrier_semaphore()
    peers = [x_peer(dx)[1] for dx in range(1, NX)] + [y_peer]
    peers += [z_peer(dz)[1] for dz in range(1, NZ)]
    peers += [g_peer(k)[1] for k in range(1, group)]
    for peer in peers:
        pl.semaphore_signal(barrier, inc=1, device_id=peer, device_id_type=MESH)

    loads[0].wait()
    loads[1].wait()
    turned = jnp.transpose(input_v[...].astype(jnp.float32))
    turned = jnp.where(ids_v[...] != 0, turned, 0.0).astype(jnp.bfloat16)
    for py in range(NY):
        for px in range(NX):
            block = (px * NY + py) * rows
            inputs_t[py, px * rows : (px + 1) * rows, ds(x * tokens, tokens)] = turned[block : block + rows, :]

    loads[2].wait()
    for j in range(n_blocks):
        global_rows[:, j, :] = global_v[:, j * BLOCK : (j + 1) * BLOCK]
    loads[3].wait()
    delta = global_rows[...].reshape(n_rows, BLOCK) - local_v[...]
    scale = (jnp.max(jnp.abs(delta), axis=1, keepdims=True) + EPS).astype(jnp.bfloat16).astype(jnp.float32)
    codes = (delta / scale).astype(jnp.bfloat16)
    values[...] = (codes.astype(jnp.float32) * scale).astype(jnp.bfloat16)

    pl.semaphore_wait(barrier, len(peers))

    sends = []

    def send(src, dst, send_sem, recv_sem, device):
        copy = pltpu.make_async_remote_copy(
            src_ref=src, dst_ref=dst, send_sem=send_sem, recv_sem=recv_sem, device_id=device, device_id_type=MESH
        )
        copy.start()
        sends.append(copy)
        return copy

    a1 = []
    for dz in range(1, NZ):
        pz, device = z_peer(dz)
        a1.append(send(values.at[ds(pz * rz, rz), :], part1.at[z], a1_send.at[dz], a1_recv.at[dz], device))
    ls = []
    for dx in range(1, NX):
        px, device = x_peer(dx)
        mine = inputs_t.at[:, :, ds(x * tokens, tokens)]
        ls.append(send(mine, mine, l_send.at[dx], l_recv.at[dx], device))

    gs = [[] for _ in range(CHUNKS)]

    def send_grads(c):
        for dx in range(1, NX):
            px, device = x_peer(dx)
            gs[c].append(
                send(
                    grad_hbm.at[:, ds(px * cols + c * w, w)],
                    grads.at[ds(x * tokens, tokens), c * w : (c + 1) * w],
                    g_send.at[c, dx], g_recv.at[c, dx], device,
                )
            )

    for c in range(CHUNKS):
        send_grads(c)

    def reduce_z():
        part1[z] = values[ds(z * rz, rz), :]
        for copy in a1:
            copy.wait_recv()
        part2[g_me] = jnp.sum(part1[...].astype(jnp.float32), axis=0)
        return [
            send(part2.at[g_me], part2.at[g_me], a2_send.at[k], a2_recv.at[k], g_peer(k)[1]) for k in range(1, group)
        ]

    def reduce_group(a2):
        for copy in a2:
            copy.wait_recv()
        mine = average.at[ds(z * rz, rz), :]
        mine[...] = jnp.sum(part2[...], axis=0) / float(NZ * group)
        return [send(mine, mine, a3_send.at[dz], a3_recv.at[dz], z_peer(dz)[1]) for dz in range(1, NZ)]

    def outer_update(a3):
        for copy in a3:
            copy.wait_recv()
        loads[4].wait()
        global_rows[...] = average[...].reshape(frag, n_blocks, BLOCK)
        for j in range(n_blocks):
            at = slice(j * BLOCK, (j + 1) * BLOCK)
            mean = global_rows[:, j, :]
            fresh = MU * momentum_v[:, at] + mean
            new_momentum_ref[:, at] = fresh
            new_global_ref[:, at] = global_v[:, at] - LR * (mean + MU * fresh)

    ys, outs = [], []

    def multiply(c):
        at = slice(c * w, (c + 1) * w)
        if c == 0:
            own_grads.wait()
            for copy in ls:
                copy.wait_recv()
        for copy in gs[c]:
            copy.wait_recv()
        block = grads[:, at]
        y_out[c] = jnp.dot(inputs_t[1 - y], block, preferred_element_type=jnp.float32).astype(jnp.bfloat16)
        ys.append(send(y_out.at[c], y_in.at[c], y_send.at[c], y_recv.at[c], y_peer))
        own_half[c % 2] = jnp.dot(inputs_t[y], block, preferred_element_type=jnp.float32)

    stores = []

    def finish(c):
        ys[c].wait_recv()
        done[c] = (own_half[c % 2] + y_in[c].astype(jnp.float32)).astype(jnp.bfloat16)
        to = ds(x * cols + c * w, w)
        for dx in range(1, NX):
            px, device = x_peer(dx)
            outs.append(send(done.at[c, ds(px * rows, rows), :], out_ref.at[:, to], o_send.at[c, dx], o_recv.at[c, dx], device))
        store = pltpu.make_async_copy(done.at[c, ds(x * rows, rows), :], out_ref.at[:, to], store_sem.at[c])
        store.start()
        stores.append(store)

    a2 = reduce_z()
    a3 = None
    for c in range(CHUNKS):
        multiply(c)
        if c == 0:
            a3 = reduce_group(a2)
        else:
            finish(c - 1)
    outer_update(a3)
    finish(CHUNKS - 1)

    for copy in outs:
        copy.wait_recv()
    for copy in stores:
        copy.wait()
    for copy in sends:
        copy.wait_send()


def local(dims, local_params, global_params, momentum, layer_input, output_grad, token_ids):
    frag, d = global_params.shape
    tokens, r_in = layer_input.shape[1:]
    n_rows = frag * d // BLOCK
    nz, group = dims[1], dims[0] * dims[2]
    half, cols, rows = r_in // NY, d // NX, r_in // (NX * NY)
    w = cols // CHUNKS
    f32, bf16 = jnp.float32, jnp.bfloat16
    dma = pltpu.SemaphoreType.DMA
    anywhere = pl.BlockSpec(memory_space=pl.ANY)
    vmem = pl.BlockSpec(memory_space=pltpu.VMEM)
    new_global, new_momentum, inner_grad = pl.pallas_call(
        functools.partial(kernel, dims),
        out_shape=(
            jax.ShapeDtypeStruct((frag, d), f32),
            jax.ShapeDtypeStruct((frag, d), f32),
            jax.ShapeDtypeStruct((rows, d), bf16),
        ),
        in_specs=[anywhere] * 6,
        out_specs=(vmem, vmem, anywhere),
        scratch_shapes=[
            pltpu.VMEM((n_rows, BLOCK), f32),
            pltpu.VMEM((frag, d), f32),
            pltpu.VMEM((frag, d), f32),
            pltpu.VMEM((tokens, r_in), bf16),
            pltpu.VMEM((1, tokens), jnp.int32),
            pltpu.VMEM((frag, d // BLOCK, BLOCK), f32),
            pltpu.VMEM((n_rows, BLOCK), bf16),
            pltpu.VMEM((nz, n_rows // nz, BLOCK), bf16),
            pltpu.VMEM((group, n_rows // nz, BLOCK), f32),
            pltpu.VMEM((n_rows, BLOCK), f32),
            pltpu.VMEM((NY, half, NX * tokens), bf16),
            pltpu.VMEM((NX * tokens, cols), bf16),
            pltpu.VMEM((CHUNKS, half, w), bf16),
            pltpu.VMEM((CHUNKS, half, w), bf16),
            pltpu.VMEM((2, half, w), f32),
            pltpu.VMEM((CHUNKS, half, w), bf16),
            dma((5,)), dma(()), dma((CHUNKS,)),
            dma((NX,)), dma((NX,)),
            dma((CHUNKS, NX)), dma((CHUNKS, NX)),
            dma((CHUNKS,)), dma((CHUNKS,)),
            dma((CHUNKS, NX)), dma((CHUNKS, NX)),
            dma((nz,)), dma((nz,)),
            dma((group,)), dma((group,)),
            dma((nz,)), dma((nz,)),
        ],
        compiler_params=pltpu.CompilerParams(
            collective_id=0, has_side_effects=True, vmem_limit_bytes=32 * 1024 * 1024
        ),
    )(
        local_params.reshape(n_rows, BLOCK),
        global_params,
        momentum,
        layer_input[0],
        output_grad[0],
        token_ids,
    )
    return new_global, new_momentum, inner_grad[None]


def build(mesh, dims):
    return jax.shard_map(
        functools.partial(local, dims),
        mesh=mesh,
        in_specs=(
            P("replica", "fsdp", None),
            P("fsdp", None),
            P("fsdp", None),
            P("replica", "fsdp", None),
            P("replica", "fsdp", None),
            P("replica", "fsdp"),
        ),
        out_specs=(P("fsdp", None), P("fsdp", None), P("replica", "fsdp", None)),
        check_vma=False,
    )


def solution(mesh):
    return build(mesh, (4, 12, 2))
```

```python
import functools

import jax
import jax.numpy as jnp
from jax import lax
from jax.experimental import pallas as pl
from jax.experimental.pallas import tpu as pltpu
from jax.sharding import PartitionSpec as P

EPS = 1e-06
MU = 0.9
LR = 0.7
MESH = pl.DeviceIdType.MESH

BLOCK = 128
NX = 4
NY = 2
CHUNKS = 8
INIT = 1
WAYS = (2, 1, 3)
EARLY_Z = 5
EARLY_STEPS, LATE_STEPS = (1, 3, 4), (0, 1, 2)


def ds(start, size):
    return pl.ds(pl.multiple_of(start, size), size)


def kernel(
    dims,
    local_hbm, global_hbm, momentum_hbm, input_hbm, grad_hbm, ids_hbm,
    new_global_ref, new_momentum_ref, out_ref,
    local_v, global_v, momentum_v, input_v, ids_v,
    global_rows, values, part1, part2, average,
    inputs_t, grads, y_out, y_in, own_half, done,
    load_sem, own_sem, store_sem,
    go_sem, far_sem,
    l_send, l_recv, g_send, g_recv, y_send, y_recv, o_send, o_recv,
    a1_send, a1_recv, a2_send, a2_recv, a3_send, a3_recv,
):
    NYH, NZ, NC = dims
    replica, me = lax.axis_index("replica"), lax.axis_index("fsdp")
    x, y = lax.div(me, NY), lax.rem(me, NY)
    core = lax.rem(replica, NC)
    z = lax.rem(lax.div(replica, NC), NZ)
    yh = lax.div(replica, NC * NZ)

    tokens, d = grad_hbm.shape
    r_in = input_v.shape[1]
    rows = r_in // (NX * NY)
    half = r_in // NY
    cols = d // NX
    w = cols // CHUNKS
    n_blocks = d // BLOCK
    frag = global_v.shape[0]
    n_rows = local_v.shape[0]
    rz = n_rows // NZ

    def x_peer(dx):
        px = lax.rem(x + dx, NX)
        return px, (replica, px * NY + y)

    y_peer = (replica, x * NY + (1 - y))

    def z_peer(dz):
        pz = lax.rem(z + dz, NZ)
        return pz, ((yh * NZ + pz) * NC + core, me)

    group = NYH * NC
    g_me = yh * NC + core

    def g_peer(k):
        pk = lax.rem(g_me + k, group)
        return pk, ((lax.div(pk, NC) * NZ + z) * NC + lax.rem(pk, NC), me)

    loads = [
        pltpu.make_async_copy(src, dst, load_sem.at[i])
        for i, (src, dst) in enumerate(
            [(input_hbm, input_v), (ids_hbm, ids_v), (global_hbm, global_v), (local_hbm, local_v), (momentum_hbm, momentum_v)]
        )
    ]
    for copy in loads:
        copy.start()
    own_grads = pltpu.make_async_copy(
        grad_hbm.at[:, ds(x * cols, cols)], grads.at[ds(x * tokens, tokens), :], own_sem
    )
    own_grads.start()

    barrier = pltpu.get_barrier_semaphore()
    first, second = replica - core, replica - core + 1
    near = [lax.rem(x + dx, NX) * NY + y for dx in range(1, NX)] + [x * NY + (1 - y)]
    for peer in near:
        pl.semaphore_signal(barrier, inc=1, device_id=(first, peer), device_id_type=MESH)

    @pl.when(core == 1)
    def _():
        pl.semaphore_signal(barrier, inc=1, device_id=(first, me), device_id_type=MESH)

    @pl.when(core == 0)
    def _():
        pl.semaphore_wait(barrier, NC * len(near) + 1)
        pl.semaphore_signal(go_sem, inc=1, device_id=(second, me), device_id_type=MESH)

    @pl.when(core == 1)
    def _():
        pl.semaphore_wait(go_sem, 1)

    sends = []

    def remote(src, dst, send_sem, recv_sem, device):
        copy = pltpu.make_async_remote_copy(
            src_ref=src, dst_ref=dst, send_sem=send_sem, recv_sem=recv_sem, device_id=device, device_id_type=MESH
        )
        sends.append(copy)
        return copy

    def send(*operands):
        copy = remote(*operands)
        copy.start()
        return copy

    gs = [[] for _ in range(CHUNKS)]

    def send_grads(c):
        for dx in range(1, NX):
            px, device = x_peer(dx)
            gs[c].append(
                send(
                    grad_hbm.at[:, ds(px * cols + c * w, w)],
                    grads.at[ds(x * tokens, tokens), c * w : (c + 1) * w],
                    g_send.at[c, dx], g_recv.at[c, dx], device,
                )
            )

    for c in range(INIT):
        send_grads(c)

    loads[0].wait()
    loads[1].wait()
    turned = jnp.transpose(input_v[...].astype(jnp.float32))
    turned = jnp.where(ids_v[...] != 0, turned, 0.0).astype(jnp.bfloat16)
    for py in range(NY):
        for px in range(NX):
            block = (px * NY + py) * rows
            inputs_t[py, px * rows : (px + 1) * rows, ds(x * tokens, tokens)] = turned[block : block + rows, :]

    mine = inputs_t.at[:, :, ds(x * tokens, tokens)]
    ls = [send(mine, mine, l_send.at[i], l_recv.at[i], x_peer(dx)[1]) for i, dx in enumerate(WAYS)]
    for c in range(INIT, CHUNKS):
        send_grads(c)

    @pl.when(core == 1)
    def _():
        for dz in range(1, NZ):
            pl.semaphore_signal(barrier, inc=1, device_id=z_peer(dz)[1], device_id_type=MESH)
        for dy in range(1, NYH):
            peer = ((lax.rem(yh + dy, NYH) * NZ + z) * NC + core, me)
            pl.semaphore_signal(barrier, inc=1, device_id=peer, device_id_type=MESH)

    loads[2].wait()
    for j in range(n_blocks):
        global_rows[:, j, :] = global_v[:, j * BLOCK : (j + 1) * BLOCK]
    loads[3].wait()
    delta = global_rows[...].reshape(n_rows, BLOCK) - local_v[...]
    scale = (jnp.max(jnp.abs(delta), axis=1, keepdims=True) + EPS).astype(jnp.bfloat16).astype(jnp.float32)
    codes = (delta / scale).astype(jnp.bfloat16)
    values[...] = (codes.astype(jnp.float32) * scale).astype(jnp.bfloat16)

    a1, a2, a3 = [], [], []
    mean_rows = average.at[ds(z * rz, rz), :]
    for dz in range(1, NZ):
        pz, device = z_peer(dz)
        a1.append(remote(values.at[ds(pz * rz, rz), :], part1.at[z], a1_send.at[dz], a1_recv.at[dz], device))
        a3.append(remote(mean_rows, mean_rows, a3_send.at[dz], a3_recv.at[dz], device))
    for k in range(1, group):
        a2.append(remote(part2.at[g_me], part2.at[g_me], a2_send.at[k], a2_recv.at[k], g_peer(k)[1]))

    def meet_far():
        @pl.when(core == 1)
        def _():
            pl.semaphore_wait(barrier, NZ - 1 + NYH - 1)
            pl.semaphore_signal(far_sem, inc=1, device_id=(first, me), device_id_type=MESH)

        @pl.when(core == 0)
        def _():
            pl.semaphore_wait(far_sem, 1)

        for copy in a1:
            copy.start()

    def reduce_z():
        part1[z] = values[ds(z * rz, rz), :]
        for copy in a1:
            copy.wait_recv()
        part2[g_me] = jnp.sum(part1[...].astype(jnp.float32), axis=0)
        for copy in a2:
            copy.start()

    def reduce_group():
        for copy in a2:
            copy.wait_recv()
        mean_rows[...] = jnp.sum(part2[...], axis=0) / float(NZ * group)
        for copy in a3:
            copy.start()

    def outer_update():
        for copy in a3:
            copy.wait_recv()
        loads[4].wait()
        global_rows[...] = average[...].reshape(frag, n_blocks, BLOCK)
        for j in range(n_blocks):
            at = slice(j * BLOCK, (j + 1) * BLOCK)
            mean = global_rows[:, j, :]
            fresh = MU * momentum_v[:, at] + mean
            new_momentum_ref[:, at] = fresh
            new_global_ref[:, at] = global_v[:, at] - LR * (mean + MU * fresh)

    ys, outs = [], []

    def multiply(c):
        at = slice(c * w, (c + 1) * w)
        if c == 0:
            own_grads.wait()
            for copy in ls:
                copy.wait_recv()
        for copy in gs[c]:
            copy.wait_recv()
        block = grads[:, at]
        y_out[c] = jnp.dot(inputs_t[1 - y], block, preferred_element_type=jnp.float32).astype(jnp.bfloat16)
        ys.append(send(y_out.at[c], y_in.at[c], y_send.at[c], y_recv.at[c], y_peer))
        own_half[c % 2] = jnp.dot(inputs_t[y], block, preferred_element_type=jnp.float32)

    stores = []

    def finish(c):
        ys[c].wait_recv()
        done[c] = (own_half[c % 2] + y_in[c].astype(jnp.float32)).astype(jnp.bfloat16)
        to = ds(x * cols + c * w, w)
        for dx in range(1, NX):
            px, device = x_peer(dx)
            outs.append(send(done.at[c, ds(px * rows, rows), :], out_ref.at[:, to], o_send.at[c, dx], o_recv.at[c, dx], device))
        store = pltpu.make_async_copy(done.at[c, ds(x * rows, rows), :], out_ref.at[:, to], store_sem.at[c])
        store.start()
        stores.append(store)

    steps = (meet_far, reduce_z, reduce_group)
    early = z < EARLY_Z
    for c in range(CHUNKS):
        for at, wanted in ((EARLY_STEPS, early), (LATE_STEPS, jnp.logical_not(early))):
            if c in at:
                pl.when(wanted)(steps[at.index(c)])
        multiply(c)
        if c:
            finish(c - 1)
    outer_update()
    finish(CHUNKS - 1)

    for copy in outs:
        copy.wait_recv()
    for copy in stores:
        copy.wait()
    for copy in sends:
        copy.wait_send()


def hand_over(*refs):
    ins, outs, held, (in_sem, out_sem) = refs[:3], refs[3:6], refs[6:9], refs[9:]
    quarter = ins[2].shape[1] // 4
    views = [lambda ref, i=i: ref.at[:, pl.ds(i * quarter, quarter), :] for i in range(4)]
    moves = [(2, view) for view in views] + [(0, lambda ref: ref), (1, lambda ref: ref)]
    loads = [pltpu.make_async_copy(view(ins[k]), view(held[k]), in_sem.at[i]) for i, (k, view) in enumerate(moves)]
    stores = [pltpu.make_async_copy(view(held[k]), view(outs[k]), out_sem.at[i]) for i, (k, view) in enumerate(moves)]
    for copy in loads:
        copy.start()
    for load, store in zip(loads, stores):
        load.wait()
        store.start()
    for copy in stores:
        copy.wait()


def local(dims, local_params, global_params, momentum, layer_input, output_grad, token_ids):
    frag, d = global_params.shape
    tokens, r_in = layer_input.shape[1:]
    n_rows = frag * d // BLOCK
    nz, group = dims[1], dims[0] * dims[2]
    half, cols, rows = r_in // NY, d // NX, r_in // (NX * NY)
    w = cols // CHUNKS
    f32, bf16 = jnp.float32, jnp.bfloat16
    dma = pltpu.SemaphoreType.DMA
    anywhere = pl.BlockSpec(memory_space=pl.ANY)
    vmem = pl.BlockSpec(memory_space=pltpu.VMEM)
    new_global, new_momentum, inner_grad = pl.pallas_call(
        functools.partial(kernel, dims),
        out_shape=(
            jax.ShapeDtypeStruct((frag, d), f32),
            jax.ShapeDtypeStruct((frag, d), f32),
            jax.ShapeDtypeStruct((rows, d), bf16),
        ),
        in_specs=[anywhere] * 6,
        out_specs=(vmem, vmem, vmem),
        scratch_shapes=[
            pltpu.VMEM((n_rows, BLOCK), f32),
            pltpu.VMEM((frag, d), f32),
            pltpu.VMEM((frag, d), f32),
            pltpu.VMEM((tokens, r_in), bf16),
            pltpu.VMEM((1, tokens), jnp.int32),
            pltpu.VMEM((frag, d // BLOCK, BLOCK), f32),
            pltpu.VMEM((n_rows, BLOCK), bf16),
            pltpu.VMEM((nz, n_rows // nz, BLOCK), bf16),
            pltpu.VMEM((group, n_rows // nz, BLOCK), f32),
            pltpu.VMEM((n_rows, BLOCK), f32),
            pltpu.VMEM((NY, half, NX * tokens), bf16),
            pltpu.VMEM((NX * tokens, cols), bf16),
            pltpu.VMEM((CHUNKS, half, w), bf16),
            pltpu.VMEM((CHUNKS, half, w), bf16),
            pltpu.VMEM((2, half, w), f32),
            pltpu.VMEM((CHUNKS, half, w), bf16),
            dma((5,)), dma(()), dma((CHUNKS,)),
            pltpu.SemaphoreType.REGULAR, pltpu.SemaphoreType.REGULAR,
            dma((NX - 1,)), dma((NX - 1,)),
            dma((CHUNKS, NX)), dma((CHUNKS, NX)),
            dma((CHUNKS,)), dma((CHUNKS,)),
            dma((CHUNKS, NX)), dma((CHUNKS, NX)),
            dma((nz,)), dma((nz,)),
            dma((group,)), dma((group,)),
            dma((nz,)), dma((nz,)),
        ],
        compiler_params=pltpu.CompilerParams(
            collective_id=0, has_side_effects=True, vmem_limit_bytes=60 * 1024 * 1024
        ),
    )(
        local_params.reshape(n_rows, BLOCK),
        global_params,
        momentum,
        layer_input[0],
        output_grad[0],
        token_ids,
    )
    return pl.pallas_call(
        hand_over,
        out_shape=(
            jax.ShapeDtypeStruct((frag, d), f32),
            jax.ShapeDtypeStruct((frag, d), f32),
            jax.ShapeDtypeStruct((1, rows, d), bf16),
        ),
        in_specs=[anywhere] * 3,
        out_specs=(anywhere,) * 3,
        scratch_shapes=[pltpu.VMEM((frag, d), f32), pltpu.VMEM((frag, d), f32), pltpu.VMEM((1, rows, d), bf16), dma((6,)), dma((6,))],
        compiler_params=pltpu.CompilerParams(vmem_limit_bytes=60 * 1024 * 1024),
    )(new_global, new_momentum, inner_grad[None])


def build(mesh, dims):
    return jax.shard_map(
        functools.partial(local, dims),
        mesh=mesh,
        in_specs=(
            P("replica", "fsdp", None),
            P("fsdp", None),
            P("fsdp", None),
            P("replica", "fsdp", None),
            P("replica", "fsdp", None),
            P("replica", "fsdp"),
        ),
        out_specs=(P("fsdp", None), P("fsdp", None), P("replica", "fsdp", None)),
        check_vma=False,
    )


def solution(mesh):
    return build(mesh, (4, 12, 2))
```

```python
import functools

import jax
import jax.numpy as jnp
from jax import lax
from jax.experimental import pallas as pl
from jax.experimental.pallas import tpu as pltpu
from jax.sharding import PartitionSpec as P

EPS = 1e-06
MU = 0.9
LR = 0.7
MESH = pl.DeviceIdType.MESH

BLOCK = 128
NX = 4
NY = 2
WIDTHS = (256,) * 8
CHUNKS = len(WIDTHS)
STARTS = tuple(sum(WIDTHS[:c]) for c in range(CHUNKS))
AHEAD = 8
INIT = 1
WAYS = (2, 1, 3)
EARLY_Z = 5
EARLY_STEPS, LATE_STEPS = (1, 4, 5), (0, 2, 4)


def ds(start, size):
    return pl.ds(pl.multiple_of(start, size), size)


def kernel(
    dims,
    local_hbm, global_hbm, momentum_hbm, input_hbm, grad_hbm, ids_hbm,
    new_global_ref, new_momentum_ref, out_ref,
    local_v, global_v, momentum_v, input_v, ids_v,
    global_rows, values, part1, part2, average,
    inputs_t, grads, y_out, y_in, own_half, done,
    load_sem, own_sem, store_sem,
    go_sem, far_sem,
    l_send, l_recv, g_send, g_recv, y_send, y_recv, o_send, o_recv,
    a1_send, a1_recv, a2_send, a2_recv, a3_send, a3_recv,
):
    NYH, NZ, NC = dims
    replica, me = lax.axis_index("replica"), lax.axis_index("fsdp")
    x, y = lax.div(me, NY), lax.rem(me, NY)
    core = lax.rem(replica, NC)
    z = lax.rem(lax.div(replica, NC), NZ)
    yh = lax.div(replica, NC * NZ)

    tokens, d = grad_hbm.shape
    r_in = input_v.shape[1]
    rows = r_in // (NX * NY)
    half = r_in // NY
    cols = d // NX
    n_blocks = d // BLOCK
    frag = global_v.shape[0]
    n_rows = local_v.shape[0]
    rz = n_rows // NZ

    def x_peer(dx):
        px = lax.rem(x + dx, NX)
        return px, (replica, px * NY + y)

    y_peer = (replica, x * NY + (1 - y))

    def z_peer(dz):
        pz = lax.rem(z + dz, NZ)
        return pz, ((yh * NZ + pz) * NC + core, me)

    group = NYH * NC
    g_me = yh * NC + core

    def g_peer(k):
        pk = lax.rem(g_me + k, group)
        return pk, ((lax.div(pk, NC) * NZ + z) * NC + lax.rem(pk, NC), me)

    loads = [
        pltpu.make_async_copy(src, dst, load_sem.at[i])
        for i, (src, dst) in enumerate(
            [(input_hbm, input_v), (ids_hbm, ids_v), (global_hbm, global_v), (local_hbm, local_v), (momentum_hbm, momentum_v)]
        )
    ]
    for copy in loads:
        copy.start()
    own_grads = pltpu.make_async_copy(
        grad_hbm.at[:, ds(x * cols, cols)], grads.at[ds(x * tokens, tokens), :], own_sem
    )
    own_grads.start()

    barrier = pltpu.get_barrier_semaphore()
    for px in range(NX):

        @pl.when(jnp.logical_or(y == 0, x != px))
        def _():
            pl.semaphore_signal(barrier, inc=1, device_id=(replica, px * NY + 1), device_id_type=MESH)

    @pl.when(y == 1)
    def _():
        pl.semaphore_wait(barrier, NX * NY - 1)
        pl.semaphore_signal(go_sem, inc=1, device_id=y_peer, device_id_type=MESH)

    @pl.when(y == 0)
    def _():
        pl.semaphore_wait(go_sem, 1)

    sends = []

    def remote(src, dst, send_sem, recv_sem, device):
        copy = pltpu.make_async_remote_copy(
            src_ref=src, dst_ref=dst, send_sem=send_sem, recv_sem=recv_sem, device_id=device, device_id_type=MESH
        )
        sends.append(copy)
        return copy

    def send(*operands):
        copy = remote(*operands)
        copy.start()
        return copy

    def span(c):
        return slice(STARTS[c], STARTS[c] + WIDTHS[c])

    def column(px, c):
        return pl.ds(pl.multiple_of(px * cols + STARTS[c], BLOCK), WIDTHS[c])

    gs = [[] for _ in range(CHUNKS)]

    def send_grads(c):
        for dx in range(1, NX):
            px, device = x_peer(dx)
            gs[c].append(
                send(
                    grad_hbm.at[:, column(px, c)],
                    grads.at[ds(x * tokens, tokens), span(c)],
                    g_send.at[c, dx], g_recv.at[c, dx], device,
                )
            )

    for c in range(INIT):
        send_grads(c)

    loads[0].wait()
    loads[1].wait()
    turned = jnp.transpose(input_v[...].astype(jnp.float32))
    turned = jnp.where(ids_v[...] != 0, turned, 0.0).astype(jnp.bfloat16)
    for py in range(NY):
        for px in range(NX):
            block = (px * NY + py) * rows
            inputs_t[py, px * rows : (px + 1) * rows, ds(x * tokens, tokens)] = turned[block : block + rows, :]

    mine = inputs_t.at[:, :, ds(x * tokens, tokens)]
    ls = [send(mine, mine, l_send.at[i], l_recv.at[i], x_peer(dx)[1]) for i, dx in enumerate(WAYS)]
    for c in range(INIT, AHEAD):
        send_grads(c)

    @pl.when(y == 0)
    def _():
        for peer in [z_peer(dz)[1] for dz in range(1, NZ)] + [g_peer(k)[1] for k in range(1, group)]:
            pl.semaphore_signal(barrier, inc=1, device_id=peer, device_id_type=MESH)

    loads[2].wait()
    for j in range(n_blocks):
        global_rows[:, j, :] = global_v[:, j * BLOCK : (j + 1) * BLOCK]
    loads[3].wait()
    delta = global_rows[...].reshape(n_rows, BLOCK) - local_v[...]
    scale = (jnp.max(jnp.abs(delta), axis=1, keepdims=True) + EPS).astype(jnp.bfloat16).astype(jnp.float32)
    codes = (delta / scale).astype(jnp.bfloat16)
    values[...] = (codes.astype(jnp.float32) * scale).astype(jnp.bfloat16)

    a1, a2, a3 = [], [], []
    mean_rows = average.at[ds(z * rz, rz), :]
    for dz in range(1, NZ):
        pz, device = z_peer(dz)
        a1.append(remote(values.at[ds(pz * rz, rz), :], part1.at[z], a1_send.at[dz], a1_recv.at[dz], device))
        a3.append(remote(mean_rows, mean_rows, a3_send.at[dz], a3_recv.at[dz], device))
    for k in range(1, group):
        a2.append(remote(part2.at[g_me], part2.at[g_me], a2_send.at[k], a2_recv.at[k], g_peer(k)[1]))

    def meet_far():
        @pl.when(y == 0)
        def _():
            pl.semaphore_wait(barrier, NZ - 1 + group - 1)
            pl.semaphore_signal(far_sem, inc=1, device_id=y_peer, device_id_type=MESH)

        @pl.when(y == 1)
        def _():
            pl.semaphore_wait(far_sem, 1)

        for copy in a1:
            copy.start()

    def reduce_z():
        part1[z] = values[ds(z * rz, rz), :]
        for copy in a1:
            copy.wait_recv()
        part2[g_me] = jnp.sum(part1[...].astype(jnp.float32), axis=0)
        for copy in a2:
            copy.start()

    def reduce_group():
        for copy in a2:
            copy.wait_recv()
        mean_rows[...] = jnp.sum(part2[...], axis=0) / float(NZ * group)
        for copy in a3:
            copy.start()

    def outer_update():
        for copy in a3:
            copy.wait_recv()
        loads[4].wait()
        global_rows[...] = average[...].reshape(frag, n_blocks, BLOCK)
        for j in range(n_blocks):
            at = slice(j * BLOCK, (j + 1) * BLOCK)
            mean = global_rows[:, j, :]
            fresh = MU * momentum_v[:, at] + mean
            new_momentum_ref[:, at] = fresh
            new_global_ref[:, at] = global_v[:, at] - LR * (mean + MU * fresh)

    ys, outs = [], []

    def multiply(c):
        at = span(c)
        if c == 0:
            own_grads.wait()
            for copy in ls:
                copy.wait_recv()
        for copy in gs[c]:
            copy.wait_recv()
        if c + AHEAD < CHUNKS:
            send_grads(c + AHEAD)
        block = grads[:, at]
        y_out[:, at] = jnp.dot(inputs_t[1 - y], block, preferred_element_type=jnp.float32).astype(jnp.bfloat16)
        ys.append(send(y_out.at[:, at], y_in.at[:, at], y_send.at[c], y_recv.at[c], y_peer))
        own_half[c % 2, :, : WIDTHS[c]] = jnp.dot(inputs_t[y], block, preferred_element_type=jnp.float32)

    stores = []

    def finish(c):
        ys[c].wait_recv()
        at, to = span(c), column(x, c)
        done[:, at] = (own_half[c % 2, :, : WIDTHS[c]] + y_in[:, at].astype(jnp.float32)).astype(jnp.bfloat16)
        for dx in range(1, NX):
            px, device = x_peer(dx)
            outs.append(send(done.at[ds(px * rows, rows), at], out_ref.at[:, to], o_send.at[c, dx], o_recv.at[c, dx], device))
        store = pltpu.make_async_copy(done.at[ds(x * rows, rows), at], out_ref.at[:, to], store_sem.at[c])
        store.start()
        stores.append(store)

    steps = (meet_far, reduce_z, reduce_group)
    early = z < EARLY_Z
    for c in range(CHUNKS):
        for at, wanted in ((EARLY_STEPS, early), (LATE_STEPS, jnp.logical_not(early))):
            for step, before in zip(steps, at):
                if before == c:
                    pl.when(wanted)(step)
        multiply(c)
        if c:
            finish(c - 1)
    finish(CHUNKS - 1)
    outer_update()

    for copy in outs:
        copy.wait_recv()
    for copy in stores:
        copy.wait()
    for copy in sends:
        copy.wait_send()


def hand_over(*refs):
    ins, outs, held, (in_sem, out_sem) = refs[:3], refs[3:6], refs[6:9], refs[9:]
    quarter = ins[2].shape[1] // 4
    views = [lambda ref, i=i: ref.at[:, pl.ds(i * quarter, quarter), :] for i in range(4)]
    moves = [(2, view) for view in views] + [(0, lambda ref: ref), (1, lambda ref: ref)]
    loads = [pltpu.make_async_copy(view(ins[k]), view(held[k]), in_sem.at[i]) for i, (k, view) in enumerate(moves)]
    stores = [pltpu.make_async_copy(view(held[k]), view(outs[k]), out_sem.at[i]) for i, (k, view) in enumerate(moves)]
    for copy in loads:
        copy.start()
    for load, store in zip(loads, stores):
        load.wait()
        store.start()
    for copy in stores:
        copy.wait()


def local(dims, local_params, global_params, momentum, layer_input, output_grad, token_ids):
    frag, d = global_params.shape
    tokens, r_in = layer_input.shape[1:]
    n_rows = frag * d // BLOCK
    nz, group = dims[1], dims[0] * dims[2]
    half, cols, rows = r_in // NY, d // NX, r_in // (NX * NY)
    f32, bf16 = jnp.float32, jnp.bfloat16
    dma = pltpu.SemaphoreType.DMA
    anywhere = pl.BlockSpec(memory_space=pl.ANY)
    vmem = pl.BlockSpec(memory_space=pltpu.VMEM)
    new_global, new_momentum, inner_grad = pl.pallas_call(
        functools.partial(kernel, dims),
        out_shape=(
            jax.ShapeDtypeStruct((frag, d), f32),
            jax.ShapeDtypeStruct((frag, d), f32),
            jax.ShapeDtypeStruct((rows, d), bf16),
        ),
        in_specs=[anywhere] * 6,
        out_specs=(vmem, vmem, vmem),
        scratch_shapes=[
            pltpu.VMEM((n_rows, BLOCK), f32),
            pltpu.VMEM((frag, d), f32),
            pltpu.VMEM((frag, d), f32),
            pltpu.VMEM((tokens, r_in), bf16),
            pltpu.VMEM((1, tokens), jnp.int32),
            pltpu.VMEM((frag, d // BLOCK, BLOCK), f32),
            pltpu.VMEM((n_rows, BLOCK), bf16),
            pltpu.VMEM((nz, n_rows // nz, BLOCK), bf16),
            pltpu.VMEM((group, n_rows // nz, BLOCK), f32),
            pltpu.VMEM((n_rows, BLOCK), f32),
            pltpu.VMEM((NY, half, NX * tokens), bf16),
            pltpu.VMEM((NX * tokens, cols), bf16),
            pltpu.VMEM((half, cols), bf16),
            pltpu.VMEM((half, cols), bf16),
            pltpu.VMEM((2, half, max(WIDTHS)), f32),
            pltpu.VMEM((half, cols), bf16),
            dma((5,)), dma(()), dma((CHUNKS,)),
            pltpu.SemaphoreType.REGULAR, pltpu.SemaphoreType.REGULAR,
            dma((NX - 1,)), dma((NX - 1,)),
            dma((CHUNKS, NX)), dma((CHUNKS, NX)),
            dma((CHUNKS,)), dma((CHUNKS,)),
            dma((CHUNKS, NX)), dma((CHUNKS, NX)),
            dma((nz,)), dma((nz,)),
            dma((group,)), dma((group,)),
            dma((nz,)), dma((nz,)),
        ],
        compiler_params=pltpu.CompilerParams(
            collective_id=0, has_side_effects=True, vmem_limit_bytes=60 * 1024 * 1024
        ),
    )(
        local_params.reshape(n_rows, BLOCK),
        global_params,
        momentum,
        layer_input[0],
        output_grad[0],
        token_ids,
    )
    return pl.pallas_call(
        hand_over,
        out_shape=(
            jax.ShapeDtypeStruct((frag, d), f32),
            jax.ShapeDtypeStruct((frag, d), f32),
            jax.ShapeDtypeStruct((1, rows, d), bf16),
        ),
        in_specs=[anywhere] * 3,
        out_specs=(anywhere,) * 3,
        scratch_shapes=[pltpu.VMEM((frag, d), f32), pltpu.VMEM((frag, d), f32), pltpu.VMEM((1, rows, d), bf16), dma((6,)), dma((6,))],
        compiler_params=pltpu.CompilerParams(vmem_limit_bytes=60 * 1024 * 1024),
    )(new_global, new_momentum, inner_grad[None])


def build(mesh, dims):
    return jax.shard_map(
        functools.partial(local, dims),
        mesh=mesh,
        in_specs=(
            P("replica", "fsdp", None),
            P("fsdp", None),
            P("fsdp", None),
            P("replica", "fsdp", None),
            P("replica", "fsdp", None),
            P("replica", "fsdp"),
        ),
        out_specs=(P("fsdp", None), P("fsdp", None), P("replica", "fsdp", None)),
        check_vma=False,
    )


def solution(mesh):
    return build(mesh, (4, 12, 2))
```

```python
import functools

import jax
import jax.numpy as jnp
from jax import lax
from jax.experimental import pallas as pl
from jax.experimental.pallas import tpu as pltpu
from jax.sharding import PartitionSpec as P

EPS = 1e-06
MU = 0.9
LR = 0.7
MESH = pl.DeviceIdType.MESH

BLOCK = 128
NX = 4
NY = 2
WIDTHS = (256,) * 8
CHUNKS = len(WIDTHS)
STARTS = tuple(sum(WIDTHS[:c]) for c in range(CHUNKS))
AHEAD = 8
INIT = 1
WAYS = (2, 1, 3)
EARLY_Z = 5
EARLY_STEPS, LATE_STEPS = (1, 4, 6), (0, 2, 4)


def ds(start, size):
    return pl.ds(pl.multiple_of(start, size), size)


def kernel(
    dims,
    local_hbm, global_hbm, momentum_hbm, input_hbm, grad_hbm, ids_hbm,
    new_global_ref, new_momentum_ref, out_ref,
    local_v, global_v, momentum_v, input_v, ids_v,
    global_rows, values, part1, part2, average,
    inputs_t, grads, y_out, y_in, own_half, done,
    load_sem, own_sem, store_sem,
    go_sem, far_sem,
    l_send, l_recv, g_send, g_recv, y_send, y_recv, o_send, o_recv,
    a1_send, a1_recv, a2_send, a2_recv, a3_send, a3_recv,
):
    NYH, NZ, NC = dims
    replica, me = lax.axis_index("replica"), lax.axis_index("fsdp")
    x, y = lax.div(me, NY), lax.rem(me, NY)
    core = lax.rem(replica, NC)
    z = lax.rem(lax.div(replica, NC), NZ)
    yh = lax.div(replica, NC * NZ)

    tokens, d = grad_hbm.shape
    r_in = input_v.shape[1]
    rows = r_in // (NX * NY)
    half = r_in // NY
    cols = d // NX
    n_blocks = d // BLOCK
    frag = global_v.shape[0]
    n_rows = local_v.shape[0]
    rz = n_rows // NZ

    def x_peer(dx):
        px = lax.rem(x + dx, NX)
        return px, (replica, px * NY + y)

    y_peer = (replica, x * NY + (1 - y))

    def z_peer(dz):
        pz = lax.rem(z + dz, NZ)
        return pz, ((yh * NZ + pz) * NC + core, me)

    group = NYH * NC
    g_me = yh * NC + core

    def g_peer(k):
        pk = lax.rem(g_me + k, group)
        return pk, ((lax.div(pk, NC) * NZ + z) * NC + lax.rem(pk, NC), me)

    loads = [
        pltpu.make_async_copy(src, dst, load_sem.at[i])
        for i, (src, dst) in enumerate(
            [(input_hbm, input_v), (ids_hbm, ids_v), (global_hbm, global_v), (local_hbm, local_v), (momentum_hbm, momentum_v)]
        )
    ]
    for copy in loads:
        copy.start()
    own_grads = pltpu.make_async_copy(
        grad_hbm.at[:, ds(x * cols, cols)], grads.at[ds(x * tokens, tokens), :], own_sem
    )
    own_grads.start()

    barrier = pltpu.get_barrier_semaphore()
    for px in range(NX):

        @pl.when(jnp.logical_or(y == 0, x != px))
        def _():
            pl.semaphore_signal(barrier, inc=1, device_id=(replica, px * NY + 1), device_id_type=MESH)

    @pl.when(y == 1)
    def _():
        pl.semaphore_wait(barrier, NX * NY - 1)
        pl.semaphore_signal(go_sem, inc=1, device_id=y_peer, device_id_type=MESH)

    @pl.when(y == 0)
    def _():
        pl.semaphore_wait(go_sem, 1)

    sends = []

    def remote(src, dst, send_sem, recv_sem, device):
        copy = pltpu.make_async_remote_copy(
            src_ref=src, dst_ref=dst, send_sem=send_sem, recv_sem=recv_sem, device_id=device, device_id_type=MESH
        )
        sends.append(copy)
        return copy

    def send(*operands):
        copy = remote(*operands)
        copy.start()
        return copy

    def span(c):
        return slice(STARTS[c], STARTS[c] + WIDTHS[c])

    def column(px, c):
        return pl.ds(pl.multiple_of(px * cols + STARTS[c], BLOCK), WIDTHS[c])

    gs = [[] for _ in range(CHUNKS)]

    def send_grads(c):
        for dx in range(1, NX):
            px, device = x_peer(dx)
            gs[c].append(
                send(
                    grad_hbm.at[:, column(px, c)],
                    grads.at[ds(x * tokens, tokens), span(c)],
                    g_send.at[c, dx], g_recv.at[c, dx], device,
                )
            )

    for c in range(INIT):
        send_grads(c)

    loads[0].wait()
    loads[1].wait()
    turned = jnp.transpose(input_v[...].astype(jnp.float32))
    turned = jnp.where(ids_v[...] != 0, turned, 0.0).astype(jnp.bfloat16)
    for py in range(NY):
        for px in range(NX):
            block = (px * NY + py) * rows
            inputs_t[py, px * rows : (px + 1) * rows, ds(x * tokens, tokens)] = turned[block : block + rows, :]

    mine = inputs_t.at[:, :, ds(x * tokens, tokens)]
    ls = [send(mine, mine, l_send.at[i], l_recv.at[i], x_peer(dx)[1]) for i, dx in enumerate(WAYS)]
    for c in range(INIT, AHEAD):
        send_grads(c)

    @pl.when(y == 0)
    def _():
        for peer in [z_peer(dz)[1] for dz in range(1, NZ)] + [g_peer(k)[1] for k in range(1, group)]:
            pl.semaphore_signal(barrier, inc=1, device_id=peer, device_id_type=MESH)

    loads[2].wait()
    for j in range(n_blocks):
        global_rows[:, j, :] = global_v[:, j * BLOCK : (j + 1) * BLOCK]
    loads[3].wait()
    delta = global_rows[...].reshape(n_rows, BLOCK) - local_v[...]
    scale = (jnp.max(jnp.abs(delta), axis=1, keepdims=True) + EPS).astype(jnp.bfloat16).astype(jnp.float32)
    codes = (delta / scale).astype(jnp.bfloat16)
    values[...] = (codes.astype(jnp.float32) * scale).astype(jnp.bfloat16)

    a1, a2, a3 = [], [], []
    mean_rows = average.at[ds(z * rz, rz), :]
    for dz in range(1, NZ):
        pz, device = z_peer(dz)
        a1.append(remote(values.at[ds(pz * rz, rz), :], part1.at[z], a1_send.at[dz], a1_recv.at[dz], device))
        a3.append(remote(mean_rows, mean_rows, a3_send.at[dz], a3_recv.at[dz], device))
    for k in range(1, group):
        a2.append(remote(part2.at[g_me], part2.at[g_me], a2_send.at[k], a2_recv.at[k], g_peer(k)[1]))

    def meet_far():
        @pl.when(y == 0)
        def _():
            pl.semaphore_wait(barrier, NZ - 1 + group - 1)
            pl.semaphore_signal(far_sem, inc=1, device_id=y_peer, device_id_type=MESH)

        @pl.when(y == 1)
        def _():
            pl.semaphore_wait(far_sem, 1)

        for copy in a1:
            copy.start()

    def reduce_z():
        part1[z] = values[ds(z * rz, rz), :]
        for copy in a1:
            copy.wait_recv()
        part2[g_me] = jnp.sum(part1[...].astype(jnp.float32), axis=0)
        for copy in a2:
            copy.start()

    def reduce_group():
        for copy in a2:
            copy.wait_recv()
        mean_rows[...] = jnp.sum(part2[...], axis=0) / float(NZ * group)
        for copy in a3:
            copy.start()

    def outer_update():
        for copy in a3:
            copy.wait_recv()
        loads[4].wait()
        global_rows[...] = average[...].reshape(frag, n_blocks, BLOCK)
        for j in range(n_blocks):
            at = slice(j * BLOCK, (j + 1) * BLOCK)
            mean = global_rows[:, j, :]
            fresh = MU * momentum_v[:, at] + mean
            new_momentum_ref[:, at] = fresh
            new_global_ref[:, at] = global_v[:, at] - LR * (mean + MU * fresh)

    ys, outs = [], []

    def multiply(c):
        at = span(c)
        if c == 0:
            own_grads.wait()
            for copy in ls:
                copy.wait_recv()
        for copy in gs[c]:
            copy.wait_recv()
        if c + AHEAD < CHUNKS:
            send_grads(c + AHEAD)
        block = grads[:, at]
        y_out[:, at] = jnp.dot(inputs_t[1 - y], block, preferred_element_type=jnp.float32).astype(jnp.bfloat16)
        ys.append(send(y_out.at[:, at], y_in.at[:, at], y_send.at[c], y_recv.at[c], y_peer))
        own_half[c % 2, :, : WIDTHS[c]] = jnp.dot(inputs_t[y], block, preferred_element_type=jnp.float32)

    stores = []

    def finish(c):
        ys[c].wait_recv()
        at, to = span(c), column(x, c)
        done[:, at] = (own_half[c % 2, :, : WIDTHS[c]] + y_in[:, at].astype(jnp.float32)).astype(jnp.bfloat16)
        for dx in range(1, NX):
            px, device = x_peer(dx)
            outs.append(send(done.at[ds(px * rows, rows), at], out_ref.at[:, to], o_send.at[c, dx], o_recv.at[c, dx], device))
        store = pltpu.make_async_copy(done.at[ds(x * rows, rows), at], out_ref.at[:, to], store_sem.at[c])
        store.start()
        stores.append(store)

    steps = (meet_far, reduce_z, reduce_group)
    early = z < EARLY_Z
    for c in range(CHUNKS):
        for at, wanted in ((EARLY_STEPS, early), (LATE_STEPS, jnp.logical_not(early))):
            for step, before in zip(steps, at):
                if before == c:
                    pl.when(wanted)(step)
        multiply(c)
        if c:
            finish(c - 1)
    finish(CHUNKS - 1)
    outer_update()

    for copy in outs:
        copy.wait_recv()
    for copy in stores:
        copy.wait()
    for copy in sends:
        copy.wait_send()


def hand_over(*refs):
    ins, outs, held, (in_sem, out_sem) = refs[:3], refs[3:6], refs[6:9], refs[9:]
    quarter = ins[2].shape[1] // 4
    views = [lambda ref, i=i: ref.at[:, pl.ds(i * quarter, quarter), :] for i in range(4)]
    moves = [(2, view) for view in views] + [(0, lambda ref: ref), (1, lambda ref: ref)]
    loads = [pltpu.make_async_copy(view(ins[k]), view(held[k]), in_sem.at[i]) for i, (k, view) in enumerate(moves)]
    stores = [pltpu.make_async_copy(view(held[k]), view(outs[k]), out_sem.at[i]) for i, (k, view) in enumerate(moves)]
    for copy in loads:
        copy.start()
    for load, store in zip(loads, stores):
        load.wait()
        store.start()
    for copy in stores:
        copy.wait()


def local(dims, local_params, global_params, momentum, layer_input, output_grad, token_ids):
    frag, d = global_params.shape
    tokens, r_in = layer_input.shape[1:]
    n_rows = frag * d // BLOCK
    nz, group = dims[1], dims[0] * dims[2]
    half, cols, rows = r_in // NY, d // NX, r_in // (NX * NY)
    f32, bf16 = jnp.float32, jnp.bfloat16
    dma = pltpu.SemaphoreType.DMA
    anywhere = pl.BlockSpec(memory_space=pl.ANY)
    vmem = pl.BlockSpec(memory_space=pltpu.VMEM)
    new_global, new_momentum, inner_grad = pl.pallas_call(
        functools.partial(kernel, dims),
        out_shape=(
            jax.ShapeDtypeStruct((frag, d), f32),
            jax.ShapeDtypeStruct((frag, d), f32),
            jax.ShapeDtypeStruct((rows, d), bf16),
        ),
        in_specs=[anywhere] * 6,
        out_specs=(vmem, vmem, vmem),
        scratch_shapes=[
            pltpu.VMEM((n_rows, BLOCK), f32),
            pltpu.VMEM((frag, d), f32),
            pltpu.VMEM((frag, d), f32),
            pltpu.VMEM((tokens, r_in), bf16),
            pltpu.VMEM((1, tokens), jnp.int32),
            pltpu.VMEM((frag, d // BLOCK, BLOCK), f32),
            pltpu.VMEM((n_rows, BLOCK), bf16),
            pltpu.VMEM((nz, n_rows // nz, BLOCK), bf16),
            pltpu.VMEM((group, n_rows // nz, BLOCK), f32),
            pltpu.VMEM((n_rows, BLOCK), f32),
            pltpu.VMEM((NY, half, NX * tokens), bf16),
            pltpu.VMEM((NX * tokens, cols), bf16),
            pltpu.VMEM((half, cols), bf16),
            pltpu.VMEM((half, cols), bf16),
            pltpu.VMEM((2, half, max(WIDTHS)), f32),
            pltpu.VMEM((half, cols), bf16),
            dma((5,)), dma(()), dma((CHUNKS,)),
            pltpu.SemaphoreType.REGULAR, pltpu.SemaphoreType.REGULAR,
            dma((NX - 1,)), dma((NX - 1,)),
            dma((CHUNKS, NX)), dma((CHUNKS, NX)),
            dma((CHUNKS,)), dma((CHUNKS,)),
            dma((CHUNKS, NX)), dma((CHUNKS, NX)),
            dma((nz,)), dma((nz,)),
            dma((group,)), dma((group,)),
            dma((nz,)), dma((nz,)),
        ],
        compiler_params=pltpu.CompilerParams(
            collective_id=0, has_side_effects=True, vmem_limit_bytes=60 * 1024 * 1024
        ),
    )(
        local_params.reshape(n_rows, BLOCK),
        global_params,
        momentum,
        layer_input[0],
        output_grad[0],
        token_ids,
    )
    return pl.pallas_call(
        hand_over,
        out_shape=(
            jax.ShapeDtypeStruct((frag, d), f32),
            jax.ShapeDtypeStruct((frag, d), f32),
            jax.ShapeDtypeStruct((1, rows, d), bf16),
        ),
        in_specs=[anywhere] * 3,
        out_specs=(anywhere,) * 3,
        scratch_shapes=[pltpu.VMEM((frag, d), f32), pltpu.VMEM((frag, d), f32), pltpu.VMEM((1, rows, d), bf16), dma((6,)), dma((6,))],
        compiler_params=pltpu.CompilerParams(vmem_limit_bytes=60 * 1024 * 1024),
    )(new_global, new_momentum, inner_grad[None])


def build(mesh, dims):
    return jax.shard_map(
        functools.partial(local, dims),
        mesh=mesh,
        in_specs=(
            P("replica", "fsdp", None),
            P("fsdp", None),
            P("fsdp", None),
            P("replica", "fsdp", None),
            P("replica", "fsdp", None),
            P("replica", "fsdp"),
        ),
        out_specs=(P("fsdp", None), P("fsdp", None), P("replica", "fsdp", None)),
        check_vma=False,
    )


def solution(mesh):
    return build(mesh, (4, 12, 2))
```
